128 devices in a mesh: dev: 128 (over x, z, y, core).
Axes of the slice: x: 4, y: 4, z: 4, core: 2. Of those that a mesh axis runs over, the one named last changes fastest.
Arguments:
- embeddings: bfloat16 [256, 128, 1280], P('dev')
- lengths: int32 [256], replicated, may hold values from 16 to 128, as said below
- pairs: int32 [128, 2], replicated, may hold values from 0 to 255, as said below
- labels: int32 [128], P('dev'), may hold values 0 or 1
- w_query: bfloat16 [1280, 1280], replicated, may hold values from -0.15625 to 0.15625
- w_key: bfloat16 [1280, 1280], replicated, may hold values from -0.15625 to 0.15625
- w_value: bfloat16 [1280, 1280], replicated, may hold values from -0.15625 to 0.15625
- w_out: bfloat16 [1280, 1280], replicated, may hold values from -0.15625 to 0.15625
- w_class: float32 [1280], replicated, may hold values from -4 to 4
Outputs:
- d_embeddings: float32 [256, 128, 1280], P('dev')
- d_weights: float32 [1280, 4, 1280], P('dev')
The draws below stay inside these ranges and needn't reach their ends.
Inputs may be any that keep to these rules, and one draw needn't show every extreme that they name: `pairs`: the two ids of a pair differ. `lengths`: some chain has exactly 128 residues.
All inputs are finite; a program needn't handle non-finite values. No bound on the sum of `labels` on one device may be relied on, other than what follows from the above.
Results may differ from the reference program's by a relative error of at most 0.013.
Values may be sent and summed in bfloat16 or wider, within the bound.
No kernel may reach another device: no remote copies, remote signals or barrier semaphores. Data moves between devices by JAX's collectives and lax.ppermute only.
A program may use at most 192 MiB of HBM per device.

```python
import jax
import jax.numpy as jnp
from jax import lax

D = 1280
HEADS = 16
L = 128
PAIR_DEV = 1
CHAINS = 256
PAIRS = 128


def draw_embeddings(key, part):
    key = jax.random.fold_in(key, 11)
    first = jax.random.fold_in(key, 0)
    values = jnp.clip(jax.random.normal(first, (CHAINS, L, D), jnp.float32), -6.0, 6.0)
    return values.astype(jnp.bfloat16)


def draw_lengths(key, part):
    key = jax.random.fold_in(key, 5)
    first, second = jax.random.split(key)
    counts = jax.random.randint(first, (CHAINS,), L // 8, L + 1, jnp.int32)
    spot = jax.random.randint(second, (), 0, CHAINS, jnp.int32)
    return counts.at[spot].set(L)


def draw_pairs(key, part):
    key = jax.random.fold_in(key, 7)
    first, second = jax.random.split(key)
    left = jax.random.randint(first, (PAIRS,), 0, CHAINS, jnp.int32)
    offset = jax.random.randint(second, (PAIRS,), 1, CHAINS, jnp.int32)
    right = (left + offset) % CHAINS
    return jnp.stack([left, right], axis=1)


def set_ends(entries, rng, smallest, largest):
    longest = entries.shape.index(max(entries.shape))
    spots = []
    for shift in (0, 1):
        where = [jax.random.randint(jax.random.fold_in(rng, axis), (), 0, length) for axis, length in enumerate(entries.shape)]
        where[longest] = (where[longest] + shift) % entries.shape[longest]
        spots.append(tuple(where))
    return entries.at[spots[0]].set(smallest).at[spots[1]].set(largest)


def normal_values(stream_key, shape, deviation, reach, held_as=jnp.bfloat16):
    drawn = deviation * jax.random.normal(stream_key, shape, jnp.float32)
    return jnp.clip(drawn, min=-reach, max=reach).astype(held_as)


def setup_inputs(seed: int = 0) -> dict:
    splits = jax.random.split(jax.random.key(seed), 10)
    return {
        "embeddings": draw_embeddings(jax.random.fold_in(splits[9], 71), 0),
        "lengths": draw_lengths(jax.random.fold_in(splits[9], 71), 0),
        "pairs": draw_pairs(jax.random.fold_in(splits[9], 71), 0),
        "labels": set_ends((jax.random.randint(splits[3], (PAIRS,), 0, 2) < 1).astype(jnp.int32), jax.random.fold_in(splits[3], 1), 0, 1),
        "w_query": normal_values(splits[4], (D, D), D ** -0.5, 0.15625),
        "w_key": normal_values(splits[5], (D, D), D ** -0.5, 0.15625),
        "w_value": normal_values(splits[6], (D, D), D ** -0.5, 0.15625),
        "w_out": normal_values(splits[7], (D, D), D ** -0.5, 0.15625),
        "w_class": normal_values(splits[8], (D,), 1.0, 4.0, jnp.float32),
    }


def attend(query, keys, values, key_lens):
    npair, sides, length, width = query.shape
    head_dim = width // HEADS
    qh = query.reshape(npair, sides, length, HEADS, head_dim).astype(jnp.float32)
    kh = keys.reshape(npair, sides, length, HEADS, head_dim).astype(jnp.float32)
    vh = values.reshape(npair, sides, length, HEADS, head_dim).astype(jnp.float32)
    scores = jnp.einsum('psqhd,pskhd->pshqk', qh, kh) * head_dim ** (-0.5)
    slots = jnp.arange(length, dtype=jnp.int32)
    key_valid = slots[None, None, None, None, :] < key_lens[:, :, None, None, None]
    scores = jnp.where(key_valid, scores, -1000000000.0)
    scores = scores - lax.optimization_barrier(jnp.max(scores, axis=-1, keepdims=True))
    expo = jnp.exp(scores)
    probs = (expo / lax.optimization_barrier(jnp.sum(expo, axis=-1, keepdims=True))).astype(jnp.bfloat16)
    context = jnp.einsum('pshqk,pskhd->psqhd', probs.astype(jnp.float32), vh)
    return context.reshape(npair, sides, length, width).astype(jnp.bfloat16)

def forward_backward(chains, chain_lens, pair_labels, w_query, w_key, w_value, w_out, w_class):
    npair, sides, length, width = chains.shape
    flat_x = chains.reshape(-1, width)
    query = jnp.dot(flat_x, w_query, preferred_element_type=jnp.float32).astype(jnp.bfloat16).reshape(chains.shape)
    keys = jnp.dot(flat_x, w_key, preferred_element_type=jnp.float32).astype(jnp.bfloat16).reshape(chains.shape)
    values = jnp.dot(flat_x, w_value, preferred_element_type=jnp.float32).astype(jnp.bfloat16).reshape(chains.shape)
    other_lens = chain_lens[:, ::-1]

    def attention(q_in, k_in, v_in):
        return attend(q_in, k_in, v_in, other_lens)
    context, attention_back = jax.vjp(attention, query, keys[:, ::-1], values[:, ::-1])
    flat_ctx = context.reshape(-1, width)
    outputs = jnp.dot(flat_ctx, w_out, preferred_element_type=jnp.float32).reshape(chains.shape)
    slots = jnp.arange(length, dtype=jnp.int32)
    valid = (slots[None, None, :] < chain_lens[:, :, None]).astype(jnp.float32)
    lens_float = chain_lens.astype(jnp.float32)
    mixed = chains.astype(jnp.float32) + outputs
    pooled = lax.optimization_barrier(jnp.sum(mixed * valid[..., None], axis=2)) / lens_float[..., None]
    logits = lax.optimization_barrier(jnp.sum(w_class[None, :] * pooled[:, 0] * pooled[:, 1], axis=-1))
    slope = jax.nn.sigmoid(logits) - pair_labels.astype(jnp.float32)
    d_pooled = slope[:, None, None] * w_class[None, None, :] * pooled[:, ::-1]
    d_mixed = valid[..., None] * (d_pooled / lens_float[..., None])[:, :, None, :]
    d_out = d_mixed.astype(jnp.bfloat16).reshape(-1, width)
    d_ctx = lax.dot_general(d_out, w_out, (((1,), (1,)), ((), ())), preferred_element_type=jnp.float32)
    d_ctx = d_ctx.astype(jnp.bfloat16).reshape(chains.shape)
    d_query, d_keys_other, d_values_other = attention_back(d_ctx)
    d_keys = d_keys_other[:, ::-1]
    d_values = d_values_other[:, ::-1]
    grads_three = jnp.concatenate([d_query.reshape(-1, width), d_keys.reshape(-1, width), d_values.reshape(-1, width)], axis=1)
    stacked = jnp.concatenate([w_query, w_key, w_value], axis=1)
    back_in = lax.dot_general(grads_three, stacked, (((1,), (1,)), ((), ())), preferred_element_type=jnp.float32)
    d_input = d_mixed + back_in.reshape(chains.shape)
    return (d_input, flat_x, grads_three, flat_ctx, d_out)

def weight_grads(flat_x, grads_three, flat_ctx, d_out):
    upper = lax.dot_general(flat_x, grads_three, (((0,), (0,)), ((), ())), preferred_element_type=jnp.float32)
    lower = lax.dot_general(flat_ctx, d_out, (((0,), (0,)), ((), ())), preferred_element_type=jnp.float32)
    joined = jnp.concatenate([upper, lower], axis=1)
    return joined.reshape(flat_x.shape[1], 4, d_out.shape[1])

def reference(embeddings, lengths, pairs, labels, w_query, w_key, w_value, w_out, w_class):
    npairs = pairs.shape[0]
    blocks = npairs // PAIR_DEV
    pair_blocks = pairs.reshape(blocks, PAIR_DEV, 2)
    label_blocks = labels.reshape(blocks, PAIR_DEV)

    def step(carry, item):
        d_emb, d_w = carry
        ids, block_labels = item
        chains = jnp.take(embeddings, ids, axis=0)
        chain_lens = jnp.take(lengths, ids, axis=0)
        d_input, flat_x, grads_three, flat_ctx, d_out = forward_backward(chains, chain_lens, block_labels, w_query, w_key, w_value, w_out, w_class)
        d_w = d_w + weight_grads(flat_x, grads_three, flat_ctx, d_out)
        d_emb = d_emb.at[ids.reshape(-1)].add(d_input.reshape(-1, L, D))
        return ((d_emb, d_w), None)
    init = (jnp.zeros((embeddings.shape[0], L, D), jnp.float32), jnp.zeros((D, 4, D), jnp.float32))
    (d_emb, d_w), _ = lax.scan(step, init, (pair_blocks, label_blocks))
    return (d_emb, d_w)
```

```python
import functools

import jax
import jax.numpy as jnp
from jax import lax
from jax.experimental import pallas as pl
from jax.experimental.pallas import tpu as pltpu
from jax.sharding import PartitionSpec as P

HEADS = 16
HD = 80
L = 128
D = 1280
NDEV = 128
WINDOWS = (0, 256, 640, 896)
WIN = 384
BF = jnp.bfloat16
F32 = jnp.float32
NN = (((1,), (0,)), ((), ()))
NT = (((1,), (1,)), ((), ()))
TN = (((0,), (0,)), ((), ()))


def mm(a, b, dims=NN):
    return lax.dot_general(a, b, dims, preferred_element_type=F32)


def iota(shape, dim):
    return lax.broadcasted_iota(jnp.int32, shape, dim)


def split(a):
    hi = a.astype(BF)
    return hi, (a - hi.astype(F32)).astype(BF)


def pair_kernel(
    lengths, pairs, label, x, wc, wq_h, wk_h, wv_h, wo_h,
    mine, other, dx, z, dv,
    wq, wk, wv, wo, q, k, p, s, u, dq, dk, dqb, dkb, sems,
):
    dev = lax.axis_index("dev")
    core = dev % 2
    loads = []
    for n, (src, dst) in enumerate(((wq_h, wq), (wk_h, wk), (wv_h, wv), (wo_h, wo))):
        load = pltpu.make_async_copy(src, dst, sems.at[n])
        load.start()
        loads.append(load)
    lens = [lengths[pairs[2 * dev]], lengths[pairs[2 * dev + 1]]]
    rows = iota((L, L), 0)
    lanes = iota((L, L), 1)
    scale = HD ** (-0.5)

    loads[0].wait()
    for n in range(5):
        cols = slice(256 * n, 256 * n + 256)
        q[:, cols] = mm(x[...], wq[:, cols]).astype(BF)
    loads[1].wait()
    for n in range(5):
        cols = slice(256 * n, 256 * n + 256)
        k[:, cols] = mm(x[...], wk[:, cols]).astype(BF)

    spans = []
    for h in range(HEADS):
        low = HD * h
        first = low // 128 * 128
        last = (low + HD - 1) // 128 * 128 + 128
        spans.append((low, first, last))

    for h, (low, first, last) in enumerate(spans):
        lane = iota((L, last - first), 1) + first
        inside = jnp.where((lane >= low) & (lane < low + HD), 1.0, 0.0).astype(BF)
        for a in range(2):
            b = 1 - a
            qt = q[L * a : L * a + L, first:last] * inside
            scores = mm(qt, k[L * b : L * b + L, first:last], NT) * scale
            scores = jnp.where(lanes < lens[b], scores, -1000000000.0)
            expo = jnp.exp(scores - jnp.max(scores, axis=1, keepdims=True))
            prob = expo / jnp.sum(expo, axis=1, keepdims=True)
            prob = jnp.where(rows < lens[a], prob, 0.0)
            p[a * HEADS + h] = prob
            s[a * HEADS + h : a * HEADS + h + 1, :] = jnp.sum(
                prob.astype(BF).astype(F32), axis=0, keepdims=True
            )

    head_lane = iota((HEADS, D), 1)
    head_row = iota((HEADS, D), 0)
    headmask = (head_lane >= HD * head_row) & (head_lane < HD * head_row + HD)
    ys = []
    for a in range(2):
        b = 1 - a
        hi, lo = split(s[a * HEADS : a * HEADS + HEADS, :])
        ys.append(mm(hi, x[L * b : L * b + L, :]) + mm(lo, x[L * b : L * b + L, :]))
    y = jnp.concatenate(ys, axis=0)
    y_hi, y_lo = split(y)
    loads[2].wait()
    t = mm(y_hi, wv[...]) + mm(y_lo, wv[...])
    pooled_ctx = [
        jnp.sum(jnp.where(headmask, t[HEADS * a : HEADS * a + HEADS, :], 0.0), axis=0, keepdims=True)
        for a in range(2)
    ]
    row8 = iota((8, D), 0)
    ctx8 = jnp.where(row8 == 0, pooled_ctx[0], jnp.where(row8 == 1, pooled_ctx[1], 0.0))
    z[...] = jnp.concatenate([y, ctx8], axis=0).astype(BF)
    mask_row = iota((8, 2 * L), 0)
    mask_lane = iota((8, 2 * L), 1)
    mask8 = ((mask_row == 0) & (mask_lane < lens[0])) | (
        (mask_row == 1) & (mask_lane >= L) & (mask_lane < L + lens[1])
    )
    x_sum = mm(jnp.where(mask8, 1.0, 0.0).astype(BF), x[...])
    ctx_hi, ctx_lo = split(ctx8)
    loads[3].wait()
    total = x_sum + mm(ctx_hi, wo[...]) + mm(ctx_lo, wo[...])
    lens_f = [n.astype(F32) for n in lens]
    pooled = [total[0:1, :] / lens_f[0], total[1:2, :] / lens_f[1]]
    logit = jnp.sum(wc[...] * pooled[0] * pooled[1], axis=1, keepdims=True)
    slope = 1.0 / (1.0 + jnp.exp(-logit)) - label[0].astype(F32)
    dvec = [slope * wc[...] * pooled[1 - a] / lens_f[a] for a in range(2)]
    dvec8 = jnp.where(row8 == 0, dvec[0], jnp.where(row8 == 1, dvec[1], 0.0)).astype(BF)
    dv[:, 0:D] = dvec[0].astype(BF)
    dv[:, D : 2 * D] = dvec[1].astype(BF)
    g = mm(dvec8, wo[...], NT).astype(BF).astype(F32)
    gm = jnp.concatenate(
        [jnp.where(headmask, g[a : a + 1, :], 0.0) for a in range(2)], axis=0
    ).astype(BF)
    gv = mm(gm, wv[...], NT)
    gv_hi, gv_lo = split(gv)
    for a in range(2):
        b = 1 - a
        part = slice(HEADS * a, HEADS * a + HEADS)
        xb = x[L * b : L * b + L, :]
        u[part, :] = mm(gv_hi[part, :], xb, NT) + mm(gv_lo[part, :], xb, NT)

    for h, (low, first, last) in enumerate(spans):
        keep = lanes + first >= low
        for a in range(2):
            b = 1 - a
            row = a * HEADS + h
            prob = p[row]
            uh = u[row : row + 1, :]
            mean = jnp.sum(prob * uh, axis=1, keepdims=True)
            ds = (prob * (uh - mean) * scale).astype(BF)
            for out, side, val in (
                (dq, a, mm(ds, k[L * b : L * b + L, first:last])),
                (dk, b, mm(ds, q[L * a : L * a + L, first:last], TN)),
            ):
                here = slice(L * side, L * side + L)
                head = val[:, 0:128]
                if low > first:
                    head = jnp.where(keep, head, out[here, first : first + 128])
                out[here, first : first + 128] = head
                if last - first > 128:
                    out[here, first + 128 : last] = val[:, 128:]

    dqb[...] = dq[...].astype(BF)
    dkb[...] = dk[...].astype(BF)
    for w, start in enumerate(WINDOWS):
        cols = slice(start, start + WIN)
        even = core == 0
        mine[w] = jnp.where(even, dq[:, cols], dk[:, cols]).astype(BF)
        other[w] = jnp.where(even, dk[:, cols], dq[:, cols]).astype(BF)

    to = iota((2 * L, 2 * L), 0)
    frm = iota((2 * L, 2 * L), 1)
    weave = jnp.where(frm == (to & 1) * L + (to >> 1), 1.0, 0.0).astype(BF)
    s_b = s[...].astype(BF)
    tall = iota((L, 256), 0)
    for n in range(5):
        cols = slice(256 * n, 256 * n + 256)
        acc = mm(dqb[...], wq[cols, :], NT) + mm(dkb[...], wk[cols, :], NT)
        sides = []
        for c in range(2):
            a = 1 - c
            part = slice(HEADS * a, HEADS * a + HEADS)
            low_rank = mm(s_b[part, :], gv_hi[part, cols], TN)
            sides.append(low_rank + jnp.where(tall < lens[c], dvec[c][:, cols], 0.0))
        acc = acc + jnp.concatenate(sides, axis=0)
        dx[:, cols] = mm(weave, acc.astype(BF)).astype(BF)


def pair_step(lengths, pairs, label, x, wc, wq, wk, wv, wo):
    smem = pl.BlockSpec(memory_space=pltpu.SMEM)
    vmem = pl.BlockSpec(memory_space=pltpu.VMEM)
    hbm = pl.BlockSpec(memory_space=pl.ANY)
    return pl.pallas_call(
        pair_kernel,
        out_shape=(
            jax.ShapeDtypeStruct((4, 2 * L, WIN), BF),
            jax.ShapeDtypeStruct((4, 2 * L, WIN), BF),
            jax.ShapeDtypeStruct((2 * L, D), BF),
            jax.ShapeDtypeStruct((40, D), BF),
            jax.ShapeDtypeStruct((1, 2 * D), BF),
        ),
        in_specs=[smem, smem, smem, vmem, vmem, hbm, hbm, hbm, hbm],
        out_specs=(vmem,) * 5,
        scratch_shapes=[pltpu.VMEM((D, D), BF)] * 4
        + [
            pltpu.VMEM((2 * L, D), BF),
            pltpu.VMEM((2 * L, D), BF),
            pltpu.VMEM((2 * HEADS, L, L), F32),
            pltpu.VMEM((2 * HEADS, L), F32),
            pltpu.VMEM((2 * HEADS, L), F32),
            pltpu.VMEM((2 * L, D), F32),
            pltpu.VMEM((2 * L, D), F32),
            pltpu.VMEM((2 * L, D), BF),
            pltpu.VMEM((2 * L, D), BF),
            pltpu.SemaphoreType.DMA((4,)),
        ],
        compiler_params=pltpu.CompilerParams(vmem_limit_bytes=40 * 1024 * 1024),
        cost_estimate=pl.CostEstimate(
            flops=12 * 10**9, bytes_accessed=18 * 10**6, transcendentals=6 * 10**5
        ),
        name="pair_step",
    )(lengths, pairs, label, x, wc, wq, wk, wv, wo)


def grads_kernel(*refs):
    xs, ms, zp, out = refs[:8], refs[8:12], refs[12], refs[13]
    for r in range(5):
        cols = slice(256 * r, 256 * r + 256)
        acc = None
        for n in range(4):
            for c in range(2):
                term = mm(xs[2 * n + c][:, cols], ms[n][c], TN)
                acc = term if acc is None else acc + term
        out[:, WIN * r : WIN * r + WIN] = acc.astype(BF)
    acc = None
    for r in range(5):
        place = iota((40, 256), 1) == iota((40, 256), 0) + 40 * r
        term = mm(zp[:, 256 * r : 256 * r + 256], jnp.where(place, 1.0, 0.0).astype(BF), TN)
        acc = term if acc is None else acc + term
    out[:, 5 * WIN :] = acc.astype(BF)


def grads_step(xs, ms, zp):
    vmem = pl.BlockSpec(memory_space=pltpu.VMEM)
    return pl.pallas_call(
        grads_kernel,
        out_shape=jax.ShapeDtypeStruct((2 * L, 5 * WIN + 256), BF),
        in_specs=[vmem] * 13,
        out_specs=vmem,
        compiler_params=pltpu.CompilerParams(vmem_limit_bytes=24 * 1024 * 1024),
        cost_estimate=pl.CostEstimate(
            flops=2 * 10**9, bytes_accessed=9 * 10**6, transcendentals=0
        ),
        name="grads_step",
    )(*xs, *ms, zp)


def final_kernel(got, dv, wo, emb, out):
    to = iota((L, 2 * L), 0)
    frm = iota((L, 2 * L), 1)
    picks = [jnp.where(frm == 2 * to + c, 1.0, 0.0).astype(BF) for c in range(2)]
    for c in range(2):
        emb[c] = mm(picks[c], got[:, 0:D])
    kind = iota((HEADS, 2 * L), 0)
    src = iota((HEADS, 2 * L), 1)
    fold = jnp.where((src & 15) == kind, 1.0, 0.0).astype(BF)
    sums = mm(fold, got[:, D : D + 5 * WIN])
    lane = iota((1, 128), 1)
    for half in range(2):
        for r in range(5):
            i = 5 * half + r
            for m in range(2):
                wins = []
                for y in range(4):
                    row = 4 * y + 2 * m + half
                    wins.append(sums[row : row + 1, WIN * r : WIN * r + WIN])
                for pair in range(2):
                    left, right = wins[2 * pair], wins[2 * pair + 1]
                    join = jnp.where(lane < 64, left[:, 256:384], right[:, 0:128])
                    line = jnp.concatenate([left[:, 0:256], join, right[:, 128:384]], axis=1)
                    out[i, m : m + 1, 640 * pair : 640 * pair + 640] = line
    head_lane = iota((HEADS, D), 1)
    head_row = iota((HEADS, D), 0)
    headmask = (head_lane >= HD * head_row) & (head_lane < HD * head_row + HD)
    ext = got[:, D + 5 * WIN :]
    dvs = [dv[:, D * a : D * a + D] for a in range(2)]
    gs = [mm(d, wo[...], NT).astype(BF) for d in dvs]
    for half in range(2):
        e = mm(picks[half], ext).astype(BF)
        by_g = [mm(e, gs[a], TN) for a in range(2)]
        by_d = [mm(e, dvs[a], TN) for a in range(2)]
        for r in range(5):
            i = 5 * half + r
            base = 40 * r
            val = sum(
                jnp.where(headmask, by_g[a][base + 16 * a : base + 16 * a + 16, :], 0.0)
                for a in range(2)
            )
            out[i, 2:3, :] = jnp.sum(val, axis=0, keepdims=True)
            out[i, 3:4, :] = (
                by_d[0][base + 32 : base + 33, :] + by_d[1][base + 33 : base + 34, :]
            )


def final_step(got, dv, wo):
    vmem = pl.BlockSpec(memory_space=pltpu.VMEM)
    return pl.pallas_call(
        final_kernel,
        out_shape=(
            jax.ShapeDtypeStruct((2, L, D), F32),
            jax.ShapeDtypeStruct((10, 4, D), F32),
        ),
        in_specs=[vmem] * 3,
        out_specs=(vmem, vmem),
        compiler_params=pltpu.CompilerParams(vmem_limit_bytes=32 * 1024 * 1024),
        cost_estimate=pl.CostEstimate(
            flops=2 * 10**9, bytes_accessed=7 * 10**6, transcendentals=0
        ),
        name="final_step",
    )(got, dv, wo)


def swap_cores(a):
    return lax.ppermute(a, "dev", [(d, d ^ 1) for d in range(NDEV)])


def shift_y(a, step):
    route = []
    for d in range(NDEV):
        y = (d >> 1) & 3
        route.append((d, (d & ~6) | (((y + step) & 3) << 1)))
    return lax.ppermute(a, "dev", route)


def exchange(a):
    got = lax.all_to_all(a.reshape(NDEV, 2, a.shape[1]), "dev", 0, 0, tiled=True)
    return got


def shards(embeddings, lengths, pairs, labels, w_query, w_key, w_value, w_out, w_class):
    dev = lax.axis_index("dev")
    y = (dev >> 1) & 3
    ids = pairs.reshape(-1)
    select = (ids[:, None] == jnp.arange(2 * NDEV, dtype=jnp.int32)[None, :]).astype(BF)
    f = iota((D, D), 0)
    to = iota((D, D), 1)
    regroup = (f == 5 * (to & 255) + (to >> 8)).astype(BF)

    spread = lax.all_to_all(embeddings.transpose(1, 0, 2), "dev", 0, 0, tiled=True)
    picked = mm(select, spread.reshape(2 * NDEV, D)).astype(BF)
    x = exchange(picked).transpose(1, 0, 2).reshape(2 * L, D)

    xp = mm(x, regroup).astype(BF)
    xs = []
    for step in range(4):
        near = xp if step == 0 else shift_y(xp, step)
        xs += [near, swap_cores(near)]

    mine, other, dx, z, dv = pair_step(
        lengths, ids, labels, x, w_class.reshape(1, D), w_query, w_key, w_value, w_out
    )
    rows = exchange(dx).reshape(2 * NDEV, D)
    dv_all = lax.all_gather(dv, "dev", axis=0, tiled=True)

    both = jnp.stack([mine, swap_cores(other)], axis=1)
    ms = []
    for step in range(4):
        piece = lax.dynamic_index_in_dim(both, (y + step) & 3, 0, keepdims=False)
        ms.append(piece if step == 0 else shift_y(piece, step))
    zp = mm(z, regroup).astype(BF)
    tail = grads_step(xs, ms, zp)

    summed = mm(select, rows, TN).astype(BF)
    last = jnp.concatenate([summed, tail], axis=1)
    got = exchange(last).reshape(2 * NDEV, last.shape[1])
    return final_step(got, dv_all, w_out)


def solution(mesh):
    placed = (P("dev", None, None), P(), P(), P("dev"), P(), P(), P(), P(), P())
    return jax.shard_map(
        shards,
        mesh=mesh,
        in_specs=placed,
        out_specs=(P("dev", None, None), P("dev", None, None)),
        check_vma=False,
    )
```

```python
import functools

import jax
import jax.numpy as jnp
from jax import lax
from jax.experimental import pallas as pl
from jax.experimental.pallas import tpu as pltpu
from jax.sharding import PartitionSpec as P

HEADS = 16
HD = 80
L = 128
D = 1280
NDEV = 128
HALF = 640
BF = jnp.bfloat16
F32 = jnp.float32
NN = (((1,), (0,)), ((), ()))
NT = (((1,), (1,)), ((), ()))
TN = (((0,), (0,)), ((), ()))


def mm(a, b, dims=NN):
    return lax.dot_general(a, b, dims, preferred_element_type=F32)


def iota(shape, dim):
    return lax.broadcasted_iota(jnp.int32, shape, dim)


def split(a):
    hi = a.astype(BF)
    return hi, (a - hi.astype(F32)).astype(BF)


def pair_kernel(
    lengths, pairs, label, x_h, wc, wq_h, wk_h, wv_h, wo_h,
    *refs,
):
    pieces_h, (dx_h, z) = refs[:4], refs[4:6]
    x, wq, wk, wv, wo, q, k, p, s, u, dqk, dqb, dkb, back, woven, pieces, dx, sems, out_sems = refs[6:]
    dev = lax.axis_index("dev")
    loads = []
    for n, (src, dst) in enumerate(((x_h, x), (wq_h, wq), (wk_h, wk), (wv_h, wv), (wo_h, wo))):
        load = pltpu.make_async_copy(src, dst, sems.at[n])
        load.start()
        loads.append(load)
    lens = [lengths[pairs[2 * dev]], lengths[pairs[2 * dev + 1]]]
    rows = iota((L, L), 0)
    lanes = iota((L, L), 1)
    scale = HD ** (-0.5)

    loads[0].wait()
    loads[1].wait()
    for n in range(5):
        cols = slice(256 * n, 256 * n + 256)
        q[:, cols] = mm(x[...], wq[:, cols]).astype(BF)
    loads[2].wait()
    for n in range(5):
        cols = slice(256 * n, 256 * n + 256)
        k[:, cols] = mm(x[...], wk[:, cols]).astype(BF)

    spans = []
    for h in range(HEADS):
        low = HD * h
        first = low // 128 * 128
        last = (low + HD - 1) // 128 * 128 + 128
        spans.append((low, first, last))

    for h, (low, first, last) in enumerate(spans):
        lane = iota((L, last - first), 1) + first
        inside = jnp.where((lane >= low) & (lane < low + HD), 1.0, 0.0).astype(BF)
        for a in range(2):
            b = 1 - a
            qt = q[L * a : L * a + L, first:last] * inside
            scores = mm(qt, k[L * b : L * b + L, first:last], NT) * scale
            scores = jnp.where(lanes < lens[b], scores, -1000000000.0)
            expo = jnp.exp(scores - jnp.max(scores, axis=1, keepdims=True))
            prob = expo / jnp.sum(expo, axis=1, keepdims=True)
            prob = jnp.where(rows < lens[a], prob, 0.0)
            p[a * HEADS + h] = prob
            s[a * HEADS + h : a * HEADS + h + 1, :] = jnp.sum(
                prob.astype(BF).astype(F32), axis=0, keepdims=True
            )

    head_lane = iota((HEADS, D), 1)
    head_row = iota((HEADS, D), 0)
    headmask = (head_lane >= HD * head_row) & (head_lane < HD * head_row + HD)
    ys = []
    for a in range(2):
        b = 1 - a
        hi, lo = split(s[a * HEADS : a * HEADS + HEADS, :])
        ys.append(mm(hi, x[L * b : L * b + L, :]) + mm(lo, x[L * b : L * b + L, :]))
    y = jnp.concatenate(ys, axis=0)
    y_hi, y_lo = split(y)
    loads[3].wait()
    t = mm(y_hi, wv[...]) + mm(y_lo, wv[...])
    pooled_ctx = [
        jnp.sum(jnp.where(headmask, t[HEADS * a : HEADS * a + HEADS, :], 0.0), axis=0, keepdims=True)
        for a in range(2)
    ]
    row8 = iota((8, D), 0)
    ctx8 = jnp.where(row8 == 0, pooled_ctx[0], jnp.where(row8 == 1, pooled_ctx[1], 0.0))
    z[...] = jnp.concatenate([y, ctx8], axis=0).astype(BF)
    mask_row = iota((8, 2 * L), 0)
    mask_lane = iota((8, 2 * L), 1)
    mask8 = ((mask_row == 0) & (mask_lane < lens[0])) | (
        (mask_row == 1) & (mask_lane >= L) & (mask_lane < L + lens[1])
    )
    x_sum = mm(jnp.where(mask8, 1.0, 0.0).astype(BF), x[...])
    ctx_hi, ctx_lo = split(ctx8)
    loads[4].wait()
    total = x_sum + mm(ctx_hi, wo[...]) + mm(ctx_lo, wo[...])
    lens_f = [n.astype(F32) for n in lens]
    pooled = [total[0:1, :] / lens_f[0], total[1:2, :] / lens_f[1]]
    logit = jnp.sum(wc[...] * pooled[0] * pooled[1], axis=1, keepdims=True)
    slope = 1.0 / (1.0 + jnp.exp(-logit)) - label[0].astype(F32)
    dvec = [slope * wc[...] * pooled[1 - a] / lens_f[a] for a in range(2)]
    dvec8 = jnp.where(row8 == 0, dvec[0], jnp.where(row8 == 1, dvec[1], 0.0)).astype(BF)
    g = mm(dvec8, wo[...], NT).astype(BF).astype(F32)
    gm = jnp.concatenate(
        [jnp.where(headmask, g[a : a + 1, :], 0.0) for a in range(2)], axis=0
    ).astype(BF)
    gv = mm(gm, wv[...], NT)
    gv_hi, gv_lo = split(gv)
    for a in range(2):
        b = 1 - a
        part = slice(HEADS * a, HEADS * a + HEADS)
        xb = x[L * b : L * b + L, :]
        u[part, :] = mm(gv_hi[part, :], xb, NT) + mm(gv_lo[part, :], xb, NT)

    for h, (low, first, last) in enumerate(spans):
        keep = lanes + first >= low
        for a in range(2):
            b = 1 - a
            row = a * HEADS + h
            prob = p[row]
            uh = u[row : row + 1, :]
            mean = jnp.sum(prob * uh, axis=1, keepdims=True)
            ds = (prob * (uh - mean) * scale).astype(BF)
            for out, side, val in (
                (0, a, mm(ds, k[L * b : L * b + L, first:last])),
                (1, b, mm(ds, q[L * a : L * a + L, first:last], TN)),
            ):
                here = slice(L * side, L * side + L)
                head = val[:, 0:128]
                if low > first:
                    head = jnp.where(keep, head, dqk[out, here, first : first + 128])
                dqk[out, here, first : first + 128] = head
                if last - first > 128:
                    dqk[out, here, first + 128 : last] = val[:, 128:]

    core = dev & 1
    side = (dev >> 1) & 1
    stores = []
    for n in range(4):
        start = pl.multiple_of((side ^ (n >> 1)) * HALF, 128)
        pieces[n] = dqk[core ^ (n & 1), :, pl.ds(start, HALF)].astype(BF)
        store = pltpu.make_async_copy(pieces.at[n], pieces_h[n], out_sems.at[n])
        store.start()
        stores.append(store)
    dqb[...] = dqk[0].astype(BF)
    dkb[...] = dqk[1].astype(BF)

    s_b = s[...].astype(BF)
    tall = iota((L, 256), 0)
    for n in range(5):
        cols = slice(256 * n, 256 * n + 256)
        acc = mm(dqb[...], wq[cols, :], NT) + mm(dkb[...], wk[cols, :], NT)
        for c in range(2):
            a = 1 - c
            part = slice(HEADS * a, HEADS * a + HEADS)
            val = acc[L * c : L * c + L, :] + mm(s_b[part, :], gv_hi[part, cols], TN)
            val = val + jnp.where(tall < lens[c], dvec[c][:, cols], 0.0)
            back[L * c : L * c + L, cols] = val
    for c in range(2):
        for half in range(2):
            row = 2 * c + half
            for n in range(5):
                cols = slice(HALF * half + L * n, HALF * half + L * n + L)
                woven[n, pl.ds(row, L, stride=8), :] = back[L * c : L * c + L, cols]
                woven[n, pl.ds(row + 4, L, stride=8), :] = jnp.broadcast_to(
                    dvec[c][:, cols], (L, L)
                )
    for n in range(4):
        part = slice(256 * n, 256 * n + 256)
        for m in range(5):
            dx[part, L * m : L * m + L] = woven[m, part, :].astype(BF)
        store = pltpu.make_async_copy(dx.at[part, :], dx_h.at[part, :], out_sems.at[4 + n])
        store.start()
        stores.append(store)
    for store in stores:
        store.wait()


def pair_step(lengths, pairs, label, x, wc, wq, wk, wv, wo):
    smem = pl.BlockSpec(memory_space=pltpu.SMEM)
    vmem = pl.BlockSpec(memory_space=pltpu.VMEM)
    hbm = pl.BlockSpec(memory_space=pl.ANY)
    return pl.pallas_call(
        pair_kernel,
        out_shape=(jax.ShapeDtypeStruct((2 * L, HALF), BF),) * 4
        + (
            jax.ShapeDtypeStruct((8 * L, HALF), BF),
            jax.ShapeDtypeStruct((40, D), BF),
        ),
        in_specs=[smem, smem, smem, hbm, vmem, hbm, hbm, hbm, hbm],
        out_specs=(hbm,) * 5 + (vmem,),
        scratch_shapes=[pltpu.VMEM((2 * L, D), BF)]
        + [pltpu.VMEM((D, D), BF)] * 4
        + [
            pltpu.VMEM((2 * L, D), BF),
            pltpu.VMEM((2 * L, D), BF),
            pltpu.VMEM((2 * HEADS, L, L), F32),
            pltpu.VMEM((2 * HEADS, L), F32),
            pltpu.VMEM((2 * HEADS, L), F32),
            pltpu.VMEM((2, 2 * L, D), F32),
            pltpu.VMEM((2 * L, D), BF),
            pltpu.VMEM((2 * L, D), BF),
            pltpu.VMEM((2 * L, D), F32),
            pltpu.VMEM((5, 8 * L, L), F32),
            pltpu.VMEM((4, 2 * L, HALF), BF),
            pltpu.VMEM((8 * L, HALF), BF),
            pltpu.SemaphoreType.DMA((5,)),
            pltpu.SemaphoreType.DMA((8,)),
        ],
        compiler_params=pltpu.CompilerParams(vmem_limit_bytes=60 * 1024 * 1024),
        cost_estimate=pl.CostEstimate(
            flops=12 * 10**9, bytes_accessed=18 * 10**6, transcendentals=6 * 10**5
        ),
        name="pair_step",
    )(lengths, pairs, label, x, wc, wq, wk, wv, wo)


def grads_kernel(*refs):
    ins, z, out_h = refs[:8], refs[8], refs[9]
    xs, ms, sums, zt, woven, out, sems, out_sems = refs[10:]
    loads = []
    for n in range(4):
        loads.append(pltpu.make_async_copy(ins[n], xs.at[n], sems.at[n]))
        loads.append(pltpu.make_async_copy(ins[4 + n], ms.at[n], sems.at[4 + n]))
    for load in loads:
        load.start()
    unit = jnp.where(iota((40, L), 0) == iota((40, L), 1), 1.0, 0.0).astype(BF)
    zt[...] = mm(z[...], unit, TN)
    for load in loads:
        load.wait()
    for n in range(5):
        cols = slice(256 * n, 256 * n + 256)
        acc = None
        for m in range(4):
            term = mm(xs[m, :, cols], ms[m], TN)
            acc = term if acc is None else acc + term
        for half in range(5):
            sums[half, cols, :] = acc[:, L * half : L * half + L]
    for i in range(10):
        pick = pl.ds(i, L, stride=10)
        for row in range(2):
            woven[i, pl.ds(row, L, stride=8), :] = jnp.zeros((L, L), F32)
        for n in range(5):
            woven[5 * (i % 2) + n, pl.ds(2 + i // 2, L, stride=8), :] = sums[n, pick, :]
        woven[i, pl.ds(7, L, stride=8), :] = zt[pick, :]
    stores = []
    for n in range(4):
        part = slice(256 * n, 256 * n + 256)
        for m in range(10):
            out[part, L * m : L * m + L] = woven[m, part, :].astype(BF)
        store = pltpu.make_async_copy(out.at[part, :], out_h.at[part, :], out_sems.at[n])
        store.start()
        stores.append(store)
    for store in stores:
        store.wait()


def grads_step(xs, ms, z):
    vmem = pl.BlockSpec(memory_space=pltpu.VMEM)
    hbm = pl.BlockSpec(memory_space=pl.ANY)
    return pl.pallas_call(
        grads_kernel,
        out_shape=jax.ShapeDtypeStruct((8 * L, D), BF),
        in_specs=[hbm] * 8 + [vmem],
        out_specs=hbm,
        scratch_shapes=[
            pltpu.VMEM((4, 2 * L, D), BF),
            pltpu.VMEM((4, 2 * L, HALF), BF),
            pltpu.VMEM((5, D, L), F32),
            pltpu.VMEM((D, L), F32),
            pltpu.VMEM((10, 8 * L, L), F32),
            pltpu.VMEM((8 * L, D), BF),
            pltpu.SemaphoreType.DMA((8,)),
            pltpu.SemaphoreType.DMA((4,)),
        ],
        compiler_params=pltpu.CompilerParams(vmem_limit_bytes=60 * 1024 * 1024),
        cost_estimate=pl.CostEstimate(
            flops=12 * 10**9, bytes_accessed=7 * 10**6, transcendentals=0
        ),
        name="grads_step",
    )(*xs, *ms, z)


def sum_kernel(rows_h, ids, tail_h, out_h, rows, tail, out, sems, out_sems):
    loads = []
    for n in range(4):
        part = (slice(256 * n, 256 * n + 256), slice(None))
        loads.append(pltpu.make_async_copy(rows_h.at[part], rows.at[part], sems.at[n]))
    for n in range(4):
        part = (slice(256 * n, 256 * n + 256), slice(None))
        loads.append(pltpu.make_async_copy(tail_h.at[part], tail.at[part], sems.at[4 + n]))
    for load in loads:
        load.start()
    chain = iota((2 * NDEV, 256), 0)
    halves = [None, None]
    for n in range(4):
        part = slice(256 * n, 256 * n + 256)
        loads[n].wait()
        for half in range(2):
            select = jnp.where(chain == ids[half : half + 1, part], 1.0, 0.0).astype(BF)
            term = mm(select, rows[part, :])
            halves[half] = term if n == 0 else halves[half] + term
    summed = jnp.concatenate(halves, axis=1).astype(BF)
    stores = []
    for n in range(4):
        part = slice(256 * n, 256 * n + 256)
        to = iota((256, 64), 0)
        frm = iota((256, 64), 1)
        weave = jnp.where(to == 8 * (frm >> 1) + (frm & 1), 1.0, 0.0).astype(BF)
        val = mm(weave, summed[64 * n : 64 * n + 64, :])
        loads[4 + n].wait()
        out[part, :] = (val + tail[part, :].astype(F32)).astype(BF)
        store = pltpu.make_async_copy(out.at[part, :], out_h.at[part, :], out_sems.at[n])
        store.start()
        stores.append(store)
    for store in stores:
        store.wait()


def sum_step(rows, ids, tail):
    vmem = pl.BlockSpec(memory_space=pltpu.VMEM)
    hbm = pl.BlockSpec(memory_space=pl.ANY)
    return pl.pallas_call(
        sum_kernel,
        out_shape=jax.ShapeDtypeStruct((8 * L, D), BF),
        in_specs=[hbm, vmem, hbm],
        out_specs=hbm,
        scratch_shapes=[
            pltpu.VMEM((8 * L, HALF), BF),
            pltpu.VMEM((8 * L, D), BF),
            pltpu.VMEM((8 * L, D), BF),
            pltpu.SemaphoreType.DMA((8,)),
            pltpu.SemaphoreType.DMA((4,)),
        ],
        compiler_params=pltpu.CompilerParams(vmem_limit_bytes=60 * 1024 * 1024),
        cost_estimate=pl.CostEstimate(
            flops=2 * 10**9, bytes_accessed=7 * 10**6, transcendentals=0
        ),
        name="sum_step",
    )(rows, ids, tail)


def vectors_kernel(rows, wo, dv, g):
    to = iota((2 * NDEV, 8 * L), 0)
    frm = iota((2 * NDEV, 8 * L), 1)
    for n in range(2):
        place = frm == 8 * (to & 127) + 4 + 2 * (to >> 7) + n
        pick = jnp.where(place, 1.0, 0.0).astype(BF)
        dv[:, HALF * n : HALF * n + HALF] = mm(pick, rows[...]).astype(BF)
    for n in range(5):
        cols = slice(256 * n, 256 * n + 256)
        g[:, cols] = mm(dv[...], wo[cols, :], NT).astype(BF)


def vectors_step(rows, wo):
    vmem = pl.BlockSpec(memory_space=pltpu.VMEM)
    return pl.pallas_call(
        vectors_kernel,
        out_shape=(jax.ShapeDtypeStruct((2 * NDEV, D), BF),) * 2,
        in_specs=[vmem] * 2,
        out_specs=(vmem,) * 2,
        compiler_params=pltpu.CompilerParams(vmem_limit_bytes=60 * 1024 * 1024),
        cost_estimate=pl.CostEstimate(
            flops=2 * 10**9, bytes_accessed=6 * 10**6, transcendentals=0
        ),
        name="vectors_step",
    )(rows, wo)


def final_kernel(got_h, dv_h, g_h, emb_h, out, got, dv, g, emb, wide, sums, sems, out_sems):
    loads = []
    for n in range(4):
        part = (slice(256 * n, 256 * n + 256), slice(None))
        loads.append(pltpu.make_async_copy(got_h.at[part], got.at[part], sems.at[n]))
    loads.append(pltpu.make_async_copy(dv_h, dv, sems.at[4]))
    loads.append(pltpu.make_async_copy(g_h, g, sems.at[5]))
    for load in loads:
        load.start()
    kind = iota((L, 256), 0)
    src = iota((L, 256), 1)
    t = src & 7
    same = (kind & 31) == (src >> 3)
    role = 4 * (t - 2) + ((src >> 3) & 3)
    want = ((kind < 64) & (t == (kind >> 5)) & same) | ((kind >= 64) & (kind < 96) & (t == 7) & same)
    want = want | ((kind >= 96) & (kind < 116) & (role == kind - 96))
    pick = jnp.where(want, 1.0, 0.0).astype(BF)
    stores = []
    for n in range(4):
        loads[n].wait()
        val = mm(pick, got[256 * n : 256 * n + 256, :])
        part = slice(32 * n, 32 * n + 32)
        for c in range(2):
            emb[c, part, :] = val[32 * c : 32 * c + 32, :]
            store = pltpu.make_async_copy(
                emb.at[c, part, :], emb_h.at[c, part, :], out_sems.at[2 * n + c]
            )
            store.start()
            stores.append(store)
        wide[part, :] = val[64:96, :].astype(BF)
        sums[...] = val[96:128, :] if n == 0 else sums[...] + val[96:128, :]
    ext = None
    for i in range(10):
        place = (iota((L, 512), 1) == iota((L, 512), 0) + 40 * i) & (iota((L, 512), 0) < 40)
        term = mm(wide[:, L * i : L * i + L], jnp.where(place, 1.0, 0.0).astype(BF))
        ext = term if ext is None else ext + term
    ext = ext.astype(BF)
    loads[4].wait()
    loads[5].wait()
    head_lane = iota((HEADS, D), 1)
    head_row = iota((HEADS, D), 0)
    headmask = (head_lane >= HD * head_row) & (head_lane < HD * head_row + HD)
    by_g = [mm(ext, g[L * a : L * a + L, :], TN) for a in range(2)]
    by_d = [mm(ext, dv[L * a : L * a + L, :], TN) for a in range(2)]
    for half in range(2):
        for r in range(5):
            i = 2 * r + half
            for m in range(2):
                for side in range(2):
                    row = 4 * r + 2 * side + m
                    out[i, m : m + 1, HALF * side : HALF * side + HALF] = sums[
                        row : row + 1, HALF * half : HALF * half + HALF
                    ]
            base = 40 * i
            val = sum(
                jnp.where(headmask, by_g[a][base + 16 * a : base + 16 * a + 16, :], 0.0)
                for a in range(2)
            )
            out[i, 2:3, :] = jnp.sum(val, axis=0, keepdims=True)
            out[i, 3:4, :] = (
                by_d[0][base + 32 : base + 33, :] + by_d[1][base + 33 : base + 34, :]
            )
    for store in stores:
        store.wait()


def final_step(got, dv, g):
    vmem = pl.BlockSpec(memory_space=pltpu.VMEM)
    hbm = pl.BlockSpec(memory_space=pl.ANY)
    return pl.pallas_call(
        final_kernel,
        out_shape=(
            jax.ShapeDtypeStruct((2, L, D), F32),
            jax.ShapeDtypeStruct((10, 4, D), F32),
        ),
        in_specs=[hbm] * 3,
        out_specs=(hbm, vmem),
        scratch_shapes=[
            pltpu.VMEM((8 * L, D), BF),
            pltpu.VMEM((2 * NDEV, D), BF),
            pltpu.VMEM((2 * NDEV, D), BF),
            pltpu.VMEM((2, L, D), F32),
            pltpu.VMEM((L, D), BF),
            pltpu.VMEM((32, D), F32),
            pltpu.SemaphoreType.DMA((6,)),
            pltpu.SemaphoreType.DMA((8,)),
        ],
        compiler_params=pltpu.CompilerParams(vmem_limit_bytes=60 * 1024 * 1024),
        cost_estimate=pl.CostEstimate(
            flops=2 * 10**9, bytes_accessed=7 * 10**6, transcendentals=0
        ),
        name="final_step",
    )(got, dv, g)


def trade(a, mask):
    return lax.ppermute(a, "dev", [(d, d ^ mask) for d in range(NDEV)])


def exchange(a, rows):
    blocks = a.reshape(NDEV, rows, a.shape[1])
    return lax.all_to_all(blocks, "dev", 0, 0, tiled=True)


def shards(embeddings, lengths, pairs, labels, w_query, w_key, w_value, w_out, w_class):
    ids = pairs.reshape(-1)
    select = (ids[:, None] == jnp.arange(2 * NDEV, dtype=jnp.int32)[None, :]).astype(BF)
    place = jnp.arange(8, dtype=jnp.int32)[None, :]
    spots = jnp.repeat(pairs, 2, axis=1)
    spots = jnp.concatenate([spots, jnp.full((NDEV, 4), -1, jnp.int32)], axis=1)
    spots = jnp.stack([jnp.where((place & 1) == n, spots, -1).reshape(-1) for n in range(2)])

    spread = lax.all_to_all(embeddings.transpose(1, 0, 2), "dev", 0, 0, tiled=True)
    picked = mm(select, spread.reshape(2 * NDEV, D)).astype(BF)
    x = exchange(picked, 2).transpose(1, 0, 2).reshape(2 * L, D)

    near, far = trade(x, 1), trade(x, 2)

    *pieces, dx, z = pair_step(
        lengths, ids, labels, x, w_class.reshape(1, D), w_query, w_key, w_value, w_out
    )
    ms = [pieces[0]] + [trade(pieces[n], n) for n in range(1, 4)]
    dx, far = lax.optimization_barrier((dx, far))
    rows = exchange(dx, 8).reshape(8 * NDEV, HALF)
    xs = [x, near, far, trade(far, 1)]
    tail = grads_step(xs, ms, z)

    last = sum_step(rows, spots, tail)
    got = exchange(last, 8).reshape(8 * NDEV, D)
    dv, g = vectors_step(rows, w_out)
    return final_step(got, dv, g)


def solution(mesh):
    placed = (P("dev", None, None), P(), P(), P("dev"), P(), P(), P(), P(), P())
    return jax.shard_map(
        shards,
        mesh=mesh,
        in_specs=placed,
        out_specs=(P("dev", None, None), P("dev", None, None)),
        check_vma=False,
    )
```

```python
import functools

import jax
import jax.numpy as jnp
from jax import lax
from jax.experimental import pallas as pl
from jax.experimental.pallas import tpu as pltpu
from jax.sharding import PartitionSpec as P

HEADS = 16
HD = 80
L = 128
D = 1280
NDEV = 128
HALF = 640
WIDE = 512
BF = jnp.bfloat16
F32 = jnp.float32
NN = (((1,), (0,)), ((), ()))
NT = (((1,), (1,)), ((), ()))
TN = (((0,), (0,)), ((), ()))


def mm(a, b, dims=NN):
    return lax.dot_general(a, b, dims, preferred_element_type=F32)


def iota(shape, dim):
    return lax.broadcasted_iota(jnp.int32, shape, dim)


def split(a):
    hi = a.astype(BF)
    return hi, (a - hi.astype(F32)).astype(BF)


def pair_kernel(
    lengths, pairs, label, x_h, wc, wq_h, wk_h, wv_h, wo_h,
    *refs,
):
    pieces_h, (dx_h, z) = refs[:4], refs[4:6]
    x, wq, wk, wv, wo, q, k, p, s, u, dqk, dqb, dkb, back, woven, pieces, dx, sems, out_sems = refs[6:]
    dev = lax.axis_index("dev")
    top, low_half = (slice(0, D // 2), slice(None)), (slice(D // 2, D), slice(None))
    loads = [[pltpu.make_async_copy(x_h, x, sems.at[0])]]
    for n, (src, dst) in enumerate(((wq_h, wq), (wk_h, wk), (wv_h, wv), (wo_h, wo))):
        loads.append(
            [
                pltpu.make_async_copy(src.at[half], dst.at[half], sems.at[2 * n + 1 + m])
                for m, half in enumerate((top, low_half))
            ]
        )

    def fetch(n):
        for load in loads[n]:
            load.start()

    def arrive(n):
        for load in loads[n]:
            load.wait()

    fetch(0)
    fetch(1)
    lens = [lengths[pairs[2 * dev]], lengths[pairs[2 * dev + 1]]]
    rows = iota((L, L), 0)
    lanes = iota((L, L), 1)
    scale = HD ** (-0.5)

    arrive(0)
    arrive(1)
    fetch(2)
    for n in range(5):
        cols = slice(256 * n, 256 * n + 256)
        q[:, cols] = mm(x[...], wq[:, cols]).astype(BF)
    arrive(2)
    fetch(3)
    fetch(4)
    for n in range(5):
        cols = slice(256 * n, 256 * n + 256)
        k[:, cols] = mm(x[...], wk[:, cols]).astype(BF)

    spans = []
    for h in range(HEADS):
        low = HD * h
        first = low // 128 * 128
        last = (low + HD - 1) // 128 * 128 + 128
        spans.append((low, first, last))

    for h, (low, first, last) in enumerate(spans):
        lane = iota((L, last - first), 1) + first
        inside = jnp.where((lane >= low) & (lane < low + HD), 1.0, 0.0).astype(BF)
        for a in range(2):
            b = 1 - a
            qt = q[L * a : L * a + L, first:last] * inside
            scores = mm(qt, k[L * b : L * b + L, first:last], NT) * scale
            scores = jnp.where(lanes < lens[b], scores, -1000000000.0)
            expo = jnp.exp(scores - jnp.max(scores, axis=1, keepdims=True))
            prob = expo / jnp.sum(expo, axis=1, keepdims=True)
            prob = jnp.where(rows < lens[a], prob, 0.0)
            p[a * HEADS + h] = prob
            s[a * HEADS + h : a * HEADS + h + 1, :] = jnp.sum(
                prob.astype(BF).astype(F32), axis=0, keepdims=True
            )

    head_lane = iota((HEADS, D), 1)
    head_row = iota((HEADS, D), 0)
    headmask = (head_lane >= HD * head_row) & (head_lane < HD * head_row + HD)
    ys = []
    for a in range(2):
        b = 1 - a
        hi, lo = split(s[a * HEADS : a * HEADS + HEADS, :])
        ys.append(mm(hi, x[L * b : L * b + L, :]) + mm(lo, x[L * b : L * b + L, :]))
    y = jnp.concatenate(ys, axis=0)
    arrive(3)
    t = mm(jnp.concatenate(split(y), axis=0), wv[...])
    t = t[0 : 2 * HEADS, :] + t[2 * HEADS :, :]
    pooled_ctx = [
        jnp.sum(jnp.where(headmask, t[HEADS * a : HEADS * a + HEADS, :], 0.0), axis=0, keepdims=True)
        for a in range(2)
    ]
    row8 = iota((8, D), 0)
    ctx8 = jnp.where(row8 == 0, pooled_ctx[0], jnp.where(row8 == 1, pooled_ctx[1], 0.0))
    z[...] = jnp.concatenate([y, ctx8], axis=0).astype(BF)
    mask_row = iota((8, 2 * L), 0)
    mask_lane = iota((8, 2 * L), 1)
    mask8 = ((mask_row == 0) & (mask_lane < lens[0])) | (
        (mask_row == 1) & (mask_lane >= L) & (mask_lane < L + lens[1])
    )
    x_sum = mm(jnp.where(mask8, 1.0, 0.0).astype(BF), x[...])
    arrive(4)
    mixed = mm(jnp.concatenate(split(ctx8), axis=0), wo[...])
    total = x_sum + mixed[0:8, :] + mixed[8:16, :]
    lens_f = [n.astype(F32) for n in lens]
    pooled = [total[0:1, :] / lens_f[0], total[1:2, :] / lens_f[1]]
    logit = jnp.sum(wc[...] * pooled[0] * pooled[1], axis=1, keepdims=True)
    slope = 1.0 / (1.0 + jnp.exp(-logit)) - label[0].astype(F32)
    dvec = [slope * wc[...] * pooled[1 - a] / lens_f[a] for a in range(2)]
    dvec8 = jnp.where(row8 == 0, dvec[0], jnp.where(row8 == 1, dvec[1], 0.0)).astype(BF)
    g = mm(dvec8, wo[...], NT).astype(BF).astype(F32)
    gm = jnp.concatenate(
        [jnp.where(headmask, g[a : a + 1, :], 0.0) for a in range(2)], axis=0
    ).astype(BF)
    gv = mm(gm, wv[...], NT)
    gv_hi, gv_lo = split(gv)
    for a in range(2):
        b = 1 - a
        part = slice(HEADS * a, HEADS * a + HEADS)
        xb = x[L * b : L * b + L, :]
        u[part, :] = mm(gv_hi[part, :], xb, NT) + mm(gv_lo[part, :], xb, NT)

    for h, (low, first, last) in enumerate(spans):
        keep = lanes + first >= low
        for a in range(2):
            b = 1 - a
            row = a * HEADS + h
            prob = p[row]
            uh = u[row : row + 1, :]
            mean = jnp.sum(prob * uh, axis=1, keepdims=True)
            ds = (prob * (uh - mean) * scale).astype(BF)
            for out, side, val in (
                (0, a, mm(ds, k[L * b : L * b + L, first:last])),
                (1, b, mm(ds, q[L * a : L * a + L, first:last], TN)),
            ):
                here = slice(L * side, L * side + L)
                head = val[:, 0:128]
                if low > first:
                    head = jnp.where(keep, head, dqk[out, here, first : first + 128])
                dqk[out, here, first : first + 128] = head
                if last - first > 128:
                    dqk[out, here, first + 128 : last] = val[:, 128:]

    core = dev & 1
    side = (dev >> 1) & 1
    stores = []
    for n in range(4):
        start = pl.multiple_of((side ^ (n >> 1)) * HALF, 128)
        pieces[n] = dqk[core ^ (n & 1), :, pl.ds(start, HALF)].astype(BF)
        store = pltpu.make_async_copy(pieces.at[n], pieces_h[n], out_sems.at[n])
        store.start()
        stores.append(store)
    dqb[...] = dqk[0].astype(BF)
    dkb[...] = dqk[1].astype(BF)

    s_b = s[...].astype(BF)
    tall = iota((L, 256), 0)
    for n in range(5):
        cols = slice(256 * n, 256 * n + 256)
        acc = mm(dqb[...], wq[cols, :], NT) + mm(dkb[...], wk[cols, :], NT)
        for c in range(2):
            a = 1 - c
            part = slice(HEADS * a, HEADS * a + HEADS)
            val = acc[L * c : L * c + L, :] + mm(s_b[part, :], gv_hi[part, cols], TN)
            val = val + jnp.where(tall < lens[c], dvec[c][:, cols], 0.0)
            back[L * c : L * c + L, cols] = val
    odd = (iota((L, D), 0) & 1) == 1
    shared = jnp.where(odd, dvec[1], dvec[0])
    for c in range(2):
        for n in range(10):
            woven[n % 4, pl.ds(3 * c + n // 4, L, stride=8), :] = back[
                L * c : L * c + L, L * n : L * n + L
            ]
    for n in range(8):
        woven[n % 4, pl.ds(6 + n // 4, L, stride=8), :] = shared[:, L * n : L * n + L]
    for n in range(2):
        woven[2 + n, pl.ds(2, L, stride=8), :] = shared[:, L * (8 + n) : L * (9 + n)]
        woven[2 + n, pl.ds(5, L, stride=8), :] = jnp.zeros((L, L), F32)
    for n in range(4):
        part = slice(256 * n, 256 * n + 256)
        for m in range(4):
            dx[part, L * m : L * m + L] = woven[m, part, :].astype(BF)
        store = pltpu.make_async_copy(dx.at[part, :], dx_h.at[part, :], out_sems.at[4 + n])
        store.start()
        stores.append(store)
    for store in stores:
        store.wait()


def pair_step(lengths, pairs, label, x, wc, wq, wk, wv, wo):
    smem = pl.BlockSpec(memory_space=pltpu.SMEM)
    vmem = pl.BlockSpec(memory_space=pltpu.VMEM)
    hbm = pl.BlockSpec(memory_space=pl.ANY)
    return pl.pallas_call(
        pair_kernel,
        out_shape=(jax.ShapeDtypeStruct((2 * L, HALF), BF),) * 4
        + (
            jax.ShapeDtypeStruct((8 * L, WIDE), BF),
            jax.ShapeDtypeStruct((40, D), BF),
        ),
        in_specs=[smem, smem, smem, hbm, vmem, hbm, hbm, hbm, hbm],
        out_specs=(hbm,) * 5 + (vmem,),
        scratch_shapes=[pltpu.VMEM((2 * L, D), BF)]
        + [pltpu.VMEM((D, D), BF)] * 4
        + [
            pltpu.VMEM((2 * L, D), BF),
            pltpu.VMEM((2 * L, D), BF),
            pltpu.VMEM((2 * HEADS, L, L), F32),
            pltpu.VMEM((2 * HEADS, L), F32),
            pltpu.VMEM((2 * HEADS, L), F32),
            pltpu.VMEM((2, 2 * L, D), F32),
            pltpu.VMEM((2 * L, D), BF),
            pltpu.VMEM((2 * L, D), BF),
            pltpu.VMEM((2 * L, D), F32),
            pltpu.VMEM((4, 8 * L, L), F32),
            pltpu.VMEM((4, 2 * L, HALF), BF),
            pltpu.VMEM((8 * L, WIDE), BF),
            pltpu.SemaphoreType.DMA((9,)),
            pltpu.SemaphoreType.DMA((8,)),
        ],
        compiler_params=pltpu.CompilerParams(vmem_limit_bytes=60 * 1024 * 1024),
        cost_estimate=pl.CostEstimate(
            flops=12 * 10**9, bytes_accessed=18 * 10**6, transcendentals=6 * 10**5
        ),
        name="pair_step",
    )(lengths, pairs, label, x, wc, wq, wk, wv, wo)


def turn_kernel(z, *refs):
    unit = jnp.where(iota((40, L), 0) == iota((40, L), 1), 1.0, 0.0).astype(BF)
    refs[-1][...] = mm(z[...], unit, TN)


def turn_step(z, ms):
    vmem = pl.BlockSpec(memory_space=pltpu.VMEM)
    hbm = pl.BlockSpec(memory_space=pl.ANY)
    return pl.pallas_call(
        turn_kernel,
        out_shape=jax.ShapeDtypeStruct((D, L), F32),
        in_specs=[vmem] + [hbm] * 3,
        out_specs=vmem,
        compiler_params=pltpu.CompilerParams(vmem_limit_bytes=60 * 1024 * 1024),
        cost_estimate=pl.CostEstimate(
            flops=12 * 10**9, bytes_accessed=7 * 10**6, transcendentals=0
        ),
        name="turn_step",
    )(z, *ms)


def merge_kernel(*refs):
    ins, zt_h, rows_h, ids, out_h = refs[:8], refs[8], refs[9], refs[10], refs[11]
    xs, ms, zt, rows, sums, woven, out, sems, out_sems = refs[12:]
    loads = []
    for n in range(4):
        loads.append(pltpu.make_async_copy(ins[n], xs.at[n], sems.at[n]))
        loads.append(pltpu.make_async_copy(ins[4 + n], ms.at[n], sems.at[4 + n]))
    loads.append(pltpu.make_async_copy(rows_h, rows, sems.at[8]))
    loads.append(pltpu.make_async_copy(zt_h, zt, sems.at[9]))
    for load in loads:
        load.start()
    for load in loads[:8]:
        load.wait()
    for n in range(5):
        cols = slice(256 * n, 256 * n + 256)
        acc = None
        for m in range(4):
            term = mm(xs[m, :, cols], ms[m], TN)
            acc = term if acc is None else acc + term
        for m in range(5):
            sums[m, cols, :] = acc[:, L * m : L * m + L]
    loads[8].wait()
    loads[9].wait()
    row = iota((2 * NDEV, 8 * L), 0)
    chain = 2 * (row & 127) + (row >> 7)
    for n in range(3):
        tiles = 4 if n < 2 else 2
        select = jnp.where(chain == ids[n : n + 1, :], 1.0, 0.0).astype(BF)
        summed = mm(select, rows[:, 0 : L * tiles])
        for c in range(2):
            for m in range(tiles):
                woven[4 * n + m, pl.ds(c, L, stride=8), :] = summed[
                    L * c : L * c + L, L * m : L * m + L
                ]
    for i in range(10):
        pick = pl.ds(i, L, stride=10)
        for n in range(5):
            woven[5 * (i % 2) + n, pl.ds(2 + i // 2, L, stride=8), :] = sums[n, pick, :]
        woven[i, pl.ds(7, L, stride=8), :] = zt[pick, :]
    stores = []
    for n in range(4):
        part = slice(256 * n, 256 * n + 256)
        for m in range(10):
            out[part, L * m : L * m + L] = woven[m, part, :].astype(BF)
        store = pltpu.make_async_copy(out.at[part, :], out_h.at[part, :], out_sems.at[n])
        store.start()
        stores.append(store)
    for store in stores:
        store.wait()


def merge_step(xs, ms, zt, rows, ids):
    vmem = pl.BlockSpec(memory_space=pltpu.VMEM)
    hbm = pl.BlockSpec(memory_space=pl.ANY)
    return pl.pallas_call(
        merge_kernel,
        out_shape=jax.ShapeDtypeStruct((8 * L, D), BF),
        in_specs=[hbm] * 10 + [vmem],
        out_specs=hbm,
        scratch_shapes=[
            pltpu.VMEM((4, 2 * L, D), BF),
            pltpu.VMEM((4, 2 * L, HALF), BF),
            pltpu.VMEM((D, L), F32),
            pltpu.VMEM((8 * L, WIDE), BF),
            pltpu.VMEM((5, D, L), F32),
            pltpu.VMEM((10, 8 * L, L), F32),
            pltpu.VMEM((8 * L, D), BF),
            pltpu.SemaphoreType.DMA((10,)),
            pltpu.SemaphoreType.DMA((4,)),
        ],
        compiler_params=pltpu.CompilerParams(vmem_limit_bytes=60 * 1024 * 1024),
        cost_estimate=pl.CostEstimate(
            flops=4 * 10**9, bytes_accessed=7 * 10**6, transcendentals=0
        ),
        name="merge_step",
    )(*xs, *ms, zt, rows, ids)


def half_kernel(rows, out):
    to = iota((L, 8 * L), 0)
    frm = iota((L, 8 * L), 1)
    picks = [jnp.where(frm == 8 * to + n, 1.0, 0.0).astype(BF) for n in (6, 7, 2)]
    out[:, 0:512] = mm(picks[0], rows[...]).astype(BF)
    out[:, 512:1024] = mm(picks[1], rows[...]).astype(BF)
    out[:, 1024:D] = mm(picks[2], rows[:, 256:512]).astype(BF)


def half_step(rows):
    vmem = pl.BlockSpec(memory_space=pltpu.VMEM)
    return pl.pallas_call(
        half_kernel,
        out_shape=jax.ShapeDtypeStruct((L, D), BF),
        in_specs=[vmem],
        out_specs=vmem,
        compiler_params=pltpu.CompilerParams(vmem_limit_bytes=60 * 1024 * 1024),
        cost_estimate=pl.CostEstimate(
            flops=10**8, bytes_accessed=10**6, transcendentals=0
        ),
        name="half_step",
    )(rows)


def vectors_kernel(own, other, wo, dv, g):
    core = lax.axis_index("dev") & 1
    dv[pl.ds(pl.multiple_of(core * L, L), L), :] = own[...]
    dv[pl.ds(pl.multiple_of((1 - core) * L, L), L), :] = other[...]
    for n in range(5):
        cols = slice(256 * n, 256 * n + 256)
        g[:, cols] = mm(dv[...], wo[cols, :], NT).astype(BF)


def vectors_step(own, other, wo):
    vmem = pl.BlockSpec(memory_space=pltpu.VMEM)
    return pl.pallas_call(
        vectors_kernel,
        out_shape=(jax.ShapeDtypeStruct((2 * NDEV, D), BF),) * 2,
        in_specs=[vmem] * 3,
        out_specs=(vmem,) * 2,
        compiler_params=pltpu.CompilerParams(vmem_limit_bytes=60 * 1024 * 1024),
        cost_estimate=pl.CostEstimate(
            flops=2 * 10**9, bytes_accessed=6 * 10**6, transcendentals=0
        ),
        name="vectors_step",
    )(own, other, wo)


def final_kernel(got, dv, g, emb_h, out, emb, wide, sums, out_sems):
    kind = iota((L, 256), 0)
    src = iota((L, 256), 1)
    t = src & 7
    same = (kind & 31) == (src >> 3)
    role = 4 * (t - 2) + ((src >> 3) & 3)
    want = ((kind < 64) & (t == (kind >> 5)) & same) | ((kind >= 64) & (kind < 96) & (t == 7) & same)
    want = want | ((kind >= 96) & (kind < 116) & (role == kind - 96))
    pick = jnp.where(want, 1.0, 0.0).astype(BF)
    stores = []
    for n in range(4):
        val = mm(pick, got[256 * n : 256 * n + 256, :])
        part = slice(32 * n, 32 * n + 32)
        for c in range(2):
            emb[c, part, :] = val[32 * c : 32 * c + 32, :]
            store = pltpu.make_async_copy(
                emb.at[c, part, :], emb_h.at[c, part, :], out_sems.at[2 * n + c]
            )
            store.start()
            stores.append(store)
        wide[part, :] = val[64:96, :].astype(BF)
        sums[...] = val[96:128, :] if n == 0 else sums[...] + val[96:128, :]
    ext = None
    for i in range(10):
        place = (iota((L, 512), 1) == iota((L, 512), 0) + 40 * i) & (iota((L, 512), 0) < 40)
        term = mm(wide[:, L * i : L * i + L], jnp.where(place, 1.0, 0.0).astype(BF))
        ext = term if ext is None else ext + term
    ext = ext.astype(BF)
    head_lane = iota((HEADS, D), 1)
    head_row = iota((HEADS, D), 0)
    headmask = (head_lane >= HD * head_row) & (head_lane < HD * head_row + HD)
    by_g = [mm(ext, g[L * a : L * a + L, :], TN) for a in range(2)]
    by_d = [mm(ext, dv[L * a : L * a + L, :], TN) for a in range(2)]
    for half in range(2):
        for r in range(5):
            i = 2 * r + half
            for m in range(2):
                for side in range(2):
                    row = 4 * r + 2 * side + m
                    out[i, m : m + 1, HALF * side : HALF * side + HALF] = sums[
                        row : row + 1, HALF * half : HALF * half + HALF
                    ]
            base = 40 * i
            val = sum(
                jnp.where(headmask, by_g[a][base + 16 * a : base + 16 * a + 16, :], 0.0)
                for a in range(2)
            )
            out[i, 2:3, :] = jnp.sum(val, axis=0, keepdims=True)
            out[i, 3:4, :] = (
                by_d[0][base + 32 : base + 33, :] + by_d[1][base + 33 : base + 34, :]
            )
    for store in stores:
        store.wait()


def final_step(got, dv, g):
    vmem = pl.BlockSpec(memory_space=pltpu.VMEM)
    hbm = pl.BlockSpec(memory_space=pl.ANY)
    return pl.pallas_call(
        final_kernel,
        out_shape=(
            jax.ShapeDtypeStruct((2, L, D), F32),
            jax.ShapeDtypeStruct((10, 4, D), F32),
        ),
        in_specs=[vmem] * 3,
        out_specs=(hbm, vmem),
        scratch_shapes=[
            pltpu.VMEM((2, L, D), F32),
            pltpu.VMEM((L, D), BF),
            pltpu.VMEM((32, D), F32),
            pltpu.SemaphoreType.DMA((8,)),
        ],
        compiler_params=pltpu.CompilerParams(vmem_limit_bytes=24 * 1024 * 1024),
        cost_estimate=pl.CostEstimate(
            flops=2 * 10**9, bytes_accessed=7 * 10**6, transcendentals=0
        ),
        name="final_step",
    )(got, dv, g)


def trade(a, mask):
    return lax.ppermute(a, "dev", [(d, d ^ mask) for d in range(NDEV)])


def exchange(a, rows):
    blocks = a.reshape(NDEV, rows, a.shape[1])
    return lax.all_to_all(blocks, "dev", 0, 0, tiled=True)


def shards(embeddings, lengths, pairs, labels, w_query, w_key, w_value, w_out, w_class):
    ids = pairs.reshape(-1)
    select = (ids[:, None] == jnp.arange(2 * NDEV, dtype=jnp.int32)[None, :]).astype(BF)
    place = jnp.arange(8, dtype=jnp.int32)[None, :]
    spots = jnp.concatenate([jnp.repeat(pairs, 3, axis=1), jnp.full((NDEV, 2), -1, jnp.int32)], axis=1)
    part = jnp.where(place < 6, place % 3, -1)
    spots = jnp.stack([jnp.where(part == n, spots, -1).reshape(-1) for n in range(3)])

    spread = lax.all_to_all(embeddings.transpose(1, 0, 2), "dev", 0, 0, tiled=True)
    picked = mm(select, spread.reshape(2 * NDEV, D)).astype(BF)
    x = exchange(picked, 2).transpose(1, 0, 2).reshape(2 * L, D)

    near, far = trade(x, 1), trade(x, 2)

    *pieces, dx, z = pair_step(
        lengths, ids, labels, x, w_class.reshape(1, D), w_query, w_key, w_value, w_out
    )
    ms = [pieces[0]] + [trade(pieces[n], n) for n in range(1, 4)]
    dx, far = lax.optimization_barrier((dx, far))
    rows = exchange(dx, 8).reshape(8 * NDEV, WIDE)
    xs = [x, near, far, trade(far, 1)]
    zt = turn_step(z, ms[1:])
    last = merge_step(xs, ms, zt, rows, spots)
    got = exchange(last, 8).reshape(8 * NDEV, D)
    own = half_step(rows)
    dv, g = vectors_step(own, trade(own, 1), w_out)
    return final_step(got, dv, g)


def solution(mesh):
    placed = (P("dev", None, None), P(), P(), P("dev"), P(), P(), P(), P(), P())
    return jax.shard_map(
        shards,
        mesh=mesh,
        in_specs=placed,
        out_specs=(P("dev", None, None), P("dev", None, None)),
        check_vma=False,
    )
```
